128 devices in a mesh: blk: 4 (over x_lo, core), shard: 32 (over z, y, x_hi).
Axes of the slice: x: 4 (x_hi: 2, x_lo: 2; x = x_hi * 2 + x_lo), y: 4, z: 4, core: 2. Of those that a mesh axis runs over, the one named last changes fastest.
Arguments:
- embeddings: bfloat16 [8, 512, 1024], P('blk', 'shard'), may hold values from -170 to 170
- centroids: bfloat16 [65536, 1024], P(('blk', 'shard')), may hold values from -6 to 6
- prices: int32 [65536], P(('blk', 'shard')), may hold values from 0 to 4095
Outputs:
- weights: float32 [8, 512, 65536], P(None, None, ('blk', 'shard'))
- centroid_sums: float32 [65536, 1024], P(('blk', 'shard'))
- loads: float32 [65536], P(('blk', 'shard'))
The draws below stay inside these ranges and needn't reach their ends.
All inputs are finite; a program needn't handle non-finite values.
Results may differ from the reference program's by a relative error of at most 0.0035.
Values may be sent and summed in bfloat16 or wider, within the bound.
No kernel may reach another device: no remote copies, remote signals or barrier semaphores. Data moves between devices by JAX's collectives and lax.ppermute only.
A program may use at most 128 MiB of HBM per device.

```python
import math
import jax
import jax.numpy as jnp
from jax import lax

D = 1024
CENT_DEV = 512
K = 65536
ROWS = 512
MB = 8


def choose_pairs(key):
    count = K // CENT_DEV
    offsets = jax.random.randint(jax.random.fold_in(key, 17), (count,), 0, CENT_DEV - 1)
    picked = jnp.arange(count, dtype=jnp.int32) * CENT_DEV + offsets
    places = jax.random.permutation(jax.random.fold_in(key, 19), MB * ROWS)[:count]
    return (picked, places)


def base_table(key):
    return jnp.clip(jax.random.normal(jax.random.fold_in(key, 11), (K, D), jnp.float32), -6.0, 6.0)


def draw_centroids(key, part):
    table = base_table(key)
    picked, places = choose_pairs(key)
    key = jax.random.fold_in(key, 2)
    count = K // CENT_DEV
    noise = jnp.clip(jax.random.normal(key, (count, D), jnp.float32), -6.0, 6.0)
    table = table.at[picked + 1].set(jnp.clip(0.991 * table[picked] + 0.134 * noise, -6.0, 6.0))
    return table.astype(jnp.bfloat16)


def draw_embeddings(key, part):
    table = base_table(key)
    picked, places = choose_pairs(key)
    key = jax.random.fold_in(key, 3)
    values = jnp.clip(jax.random.normal(key, (MB, ROWS, D), jnp.float32), -6.0, 6.0)
    count = K // CENT_DEV
    levels = jnp.array([4.0, 5.5, 7.0], jnp.float32)
    strengths = levels[jnp.arange(count) % 3]
    flat = values.reshape(MB * ROWS, D)
    flat = flat.at[places].set(strengths[:, None] * table[picked])
    return flat.reshape(MB, ROWS, D).astype(jnp.bfloat16)


def plant(values, stream_key, low, high):
    longest = values.shape.index(max(values.shape))
    spots = []
    for shift in (0, 1):
        where = [jax.random.randint(jax.random.fold_in(stream_key, axis), (), 0, length) for axis, length in enumerate(values.shape)]
        where[longest] = (where[longest] + shift) % values.shape[longest]
        spots.append(tuple(where))
    return values.at[spots[0]].set(low).at[spots[1]].set(high)


def setup_inputs(seed: int = 0) -> dict:
    streams_of = jax.random.split(jax.random.key(seed), 4)
    embeddings = draw_embeddings(jax.random.fold_in(streams_of[3], 71), 0)
    centroids = draw_centroids(jax.random.fold_in(streams_of[3], 71), 0)
    prices = plant(jax.random.randint(streams_of[2], (K,), 0, 4096), jax.random.fold_in(streams_of[2], 1), 0, 4095).astype(jnp.int32)
    return dict(embeddings=embeddings, centroids=centroids, prices=prices)


def reference(embeddings, centroids, prices):
    scale = 1.0 / math.sqrt(D)
    bias = prices.astype(jnp.float32) / 1024.0

    def one_batch(block):
        scores = jnp.dot(block, centroids.T, preferred_element_type=jnp.float32) * scale - bias
        top = lax.optimization_barrier(jnp.max(scores, axis=1, keepdims=True))
        lse = top + jnp.log(lax.optimization_barrier(jnp.sum(jnp.exp(scores - top), axis=1, keepdims=True)))
        return float(K) * jnp.exp(scores - lse)
    weights = lax.map(one_batch, embeddings)
    rounded = weights.astype(jnp.bfloat16)
    sums = jnp.dot(rounded.reshape(MB * ROWS, K).T, embeddings.reshape(MB * ROWS, D), preferred_element_type=jnp.float32)
    centroid_sums = sums / math.sqrt(MB * ROWS)
    loads = lax.optimization_barrier(jnp.sum(weights, axis=(0, 1))) / float(MB * ROWS)
    return (weights, centroid_sums, loads)
```

```python
import functools
import math

import jax
import jax.numpy as jnp
from jax import lax
from jax.experimental import pallas as pl
from jax.experimental.pallas import tpu as pltpu
from jax.sharding import PartitionSpec as P

AXES = ("blk", "shard")
SIDE = 4
LANES = 128


def place_of(device):
    blk, shard = divmod(device, 32)
    return {"x": (shard & 1) * 2 + (blk >> 1), "y": (shard >> 1) & 3, "z": shard >> 3, "c": blk & 1}


def device_at(x, y, z, c):
    return ((x & 1) * 2 + c) * 32 + z * 8 + y * 2 + (x >> 1)


def along(axis0, axis1, by):
    pairs = []
    for device in range(128):
        place = place_of(device)
        axis = axis1 if place["c"] else axis0
        place[axis] = (place[axis] + by) % SIDE
        pairs.append((device, device_at(**place)))
    return pairs


def to_core(value):
    pairs = []
    for device in range(128):
        place = place_of(device)
        place["c"] = 1 - place["c"]
        pairs.append((device, device_at(**place)))
    return lax.ppermute(value, AXES, pairs)


def shift(value, axes, by):
    return lax.ppermute(value, AXES, along(*axes, by))


ORDERS = (("x", "y"), ("y", "z"), ("z", "x"))


def spread(value, axes, here):
    out = jnp.zeros((SIDE,) + value.shape, value.dtype)
    out = lax.dynamic_update_index_in_dim(out, value, here, 0)
    for by in (2, 1, -1):
        got = shift(value, axes, by)
        out = lax.dynamic_update_index_in_dim(out, got, (here - by) % SIDE, 0)
    return out.reshape((SIDE * value.shape[0],) + value.shape[1:])


def score_kernel(scale, rows_ref, cent_ref, bias_ref, score_ref, stat_ref):
    rows = rows_ref.shape[0]
    tiles = rows // LANES
    lane = lax.broadcasted_iota(jnp.int32, (LANES, LANES), 1)
    for t in range(tiles):
        part = pl.ds(t * LANES, LANES)
        score = (
            lax.dot_general(
                rows_ref[part, :],
                cent_ref[...],
                (((1,), (1,)), ((), ())),
                preferred_element_type=jnp.float32,
            )
            * scale
            - bias_ref[...]
        )
        score_ref[part, :] = score
        top = jnp.max(score, axis=1, keepdims=True)
        total = jnp.sum(jnp.exp(score - top), axis=1, keepdims=True)
        both = jnp.where(lane == 0, top, total)
        flat = both.T
        stat_ref[t : t + 1, :] = flat[0:1, :]
        stat_ref[tiles + t : tiles + t + 1, :] = flat[1:2, :]


def score_block(rows, centroids, bias, scale):
    count, width = rows.shape
    cent = centroids.shape[0]
    return pl.pallas_call(
        functools.partial(score_kernel, scale),
        out_shape=(
            jax.ShapeDtypeStruct((count, cent), jnp.float32),
            jax.ShapeDtypeStruct((2 * count // LANES, LANES), jnp.float32),
        ),
        in_specs=[pl.BlockSpec(memory_space=pltpu.VMEM)] * 3,
        out_specs=[pl.BlockSpec(memory_space=pltpu.VMEM)] * 2,
        compiler_params=pltpu.CompilerParams(vmem_limit_bytes=24 * 2**20),
        cost_estimate=pl.CostEstimate(
            flops=2 * count * width * cent,
            bytes_accessed=2 * width * (count + cent) + 4 * count * cent,
            transcendentals=count * cent,
        ),
        name="scores",
    )(rows, centroids, bias)


def weight_kernel(
    pieces, total_cent, total_rows, where_ref, stat_a, stat_b, *refs
):
    scores = refs[:pieces]
    blocks = refs[pieces : 2 * pieces]
    out_ref, sums_ref, loads_ref = refs[2 * pieces : 2 * pieces + 3]
    staged, rounded, lse, sems = refs[2 * pieces + 3 :]
    core = where_ref[0]
    tiles = stat_a.shape[1] // 2

    top = jnp.maximum(stat_a[:, :tiles, :], stat_b[:, :tiles, :])
    total = stat_a[:, tiles:, :] * jnp.exp(stat_a[:, :tiles, :] - top) + stat_b[
        :, tiles:, :
    ] * jnp.exp(stat_b[:, :tiles, :] - top)
    lse[...] = top + jnp.log(total)

    def copies(i, kind):
        slot = i % 2
        here = where_ref[1 + i]
        if kind == 0:
            return [
                pltpu.make_async_copy(
                    staged.at[slot].reshape(4, 2, 2, 2, 16, 512).at[:, :, x_lo, j],
                    out_ref.at[x_lo, 0, j, here],
                    sems.at[slot],
                )
                for x_lo in range(2)
                for j in range(2)
            ]
        return [
            pltpu.make_async_copy(
                staged.at[slot].reshape(4, 4, 2, 16, 512).at[:, :, j],
                out_ref.at[lax.rem(here, 2), 1, j, :, :, lax.div(here, 2)],
                sems.at[slot],
            )
            for j in range(2)
        ]

    def on_kind(i, act):
        kind = core if i < pieces // 2 else 1 - core
        for k in range(2):

            @pl.when(kind == k)
            def _(k=k):
                for copy in copies(i, k):
                    act(copy)

    load = jnp.zeros((8, loads_ref.shape[1]), jnp.float32)
    for i in range(pieces):
        slot = i % 2
        if i >= 2:
            on_kind(i - 2, lambda c: c.wait())
        kind = core if i < pieces // 2 else 1 - core
        index = kind * SIDE + where_ref[1 + i]
        norm = lse[index]
        for t in range(tiles):
            part = pl.ds(t * LANES, LANES)
            column = jnp.broadcast_to(norm[t : t + 1, :], (LANES, LANES)).T
            column = jnp.concatenate([column] * (scores[i].shape[1] // LANES), axis=1)
            weight = total_cent * jnp.exp(scores[i][part, :] - column)
            staged[slot, part, :] = weight
            load = load + jnp.sum(weight.reshape(LANES // 8, 8, weight.shape[1]), axis=0)
            rounded[part, :] = weight.astype(jnp.bfloat16)
        on_kind(i, lambda c: c.start())
        part_sums = lax.dot_general(
            rounded[...],
            blocks[i][...],
            (((0,), (0,)), ((), ())),
            preferred_element_type=jnp.float32,
        )
        if i == 0:
            sums_ref[...] = part_sums
        elif i + 1 < pieces:
            sums_ref[...] += part_sums
        else:
            sums_ref[...] = (sums_ref[...] + part_sums) * (1.0 / math.sqrt(total_rows))
    loads_ref[...] = jnp.sum(load, axis=0, keepdims=True) * (1.0 / total_rows)
    on_kind(pieces - 2, lambda c: c.wait())
    on_kind(pieces - 1, lambda c: c.wait())


def weight_all(where, stat_a, stat_b, scores, blocks, total_cent, total_rows):
    pieces = len(scores)
    count, cent = scores[0].shape
    width = blocks[0].shape[1]
    vmem = pl.BlockSpec(memory_space=pltpu.VMEM)
    out, sums, loads = pl.pallas_call(
        functools.partial(weight_kernel, pieces, float(total_cent), float(total_rows)),
        out_shape=(
            jax.ShapeDtypeStruct((2, 2, 2, 4, 4, 2, 16, cent), jnp.float32),
            jax.ShapeDtypeStruct((cent, width), jnp.float32),
            jax.ShapeDtypeStruct((1, cent), jnp.float32),
        ),
        in_specs=[pl.BlockSpec(memory_space=pltpu.SMEM)] + [vmem] * (2 + 2 * pieces),
        out_specs=(pl.BlockSpec(memory_space=pl.ANY), vmem, vmem),
        scratch_shapes=[
            pltpu.VMEM((2, count, cent), jnp.float32),
            pltpu.VMEM((count, cent), jnp.bfloat16),
            pltpu.VMEM((stat_a.shape[0], stat_a.shape[1] // 2, LANES), jnp.float32),
            pltpu.SemaphoreType.DMA((2,)),
        ],
        compiler_params=pltpu.CompilerParams(vmem_limit_bytes=48 * 2**20),
        name="weights",
    )(where, stat_a, stat_b, *scores, *blocks)
    return out, sums, loads


def merged(stats):
    half = stats[0].shape[1] // 2
    tops = [s[:, :half] for s in stats]
    top = functools.reduce(jnp.maximum, tops)
    total = sum(s[:, half:] * jnp.exp(t - top) for s, t in zip(stats, tops))
    return jnp.concatenate([top, total], axis=1)


def per_device(embeddings, centroids, prices):
    blk, shard = lax.axis_index("blk"), lax.axis_index("shard")
    core = blk % 2
    at = {"x": (shard % 2) * 2 + blk // 2, "y": (shard // 2) % 4, "z": shard // 8}
    here = [jnp.where(core == 0, at[a], at[b]) for a, b in ORDERS]
    width = embeddings.shape[2]
    cent = centroids.shape[0]
    scale = 1.0 / math.sqrt(width)
    bias = (prices.astype(jnp.float32) / 1024.0).reshape(1, cent)
    total_cent = cent * 128
    total_rows = embeddings.shape[0] * embeddings.shape[1] * 128

    block = embeddings.reshape(-1, width)
    block = spread(block, ORDERS[0], here[0])
    block = spread(block, ORDERS[1], here[1])
    mine, theirs = [block], [to_core(block)]
    steps = (0, 1, -1, 2)
    for by in steps[1:]:
        got = shift(block, ORDERS[2], by)
        mine.append(got)
        theirs.append(to_core(got))
    blocks = mine + theirs
    other = jnp.where(core == 0, at["x"], at["z"])
    last = [(here[2] - by) % SIDE for by in steps] + [(other - by) % SIDE for by in steps]

    scores, stats = [], None
    for i, rows in enumerate(blocks):
        score, stat = score_block(rows, centroids, bias, scale)
        scores.append(score)
        if stats is None:
            stats = jnp.zeros((8,) + stat.shape, jnp.float32)
        kind = core if i < SIDE else 1 - core
        stats = lax.dynamic_update_index_in_dim(stats, stat, kind * SIDE + last[i], 0)
    for axes in ORDERS:
        stats = merged([stats] + [shift(stats, axes, by) for by in (2, 1, -1)])
    where = jnp.stack([core] + last).astype(jnp.int32)
    out, sums, loads = weight_all(
        where, stats, to_core(stats), scores, blocks, total_cent, total_rows
    )
    return out.reshape(8, 512, cent), sums, loads.reshape(cent)


def solution(mesh):
    placed = (P("blk", "shard", None), P(AXES, None), P(AXES))
    return jax.shard_map(
        per_device,
        mesh=mesh,
        in_specs=placed,
        out_specs=(P(None, None, AXES), P(AXES, None), P(AXES)),
        check_vma=False,
    )
```

```python
import functools
import math

import jax
import jax.numpy as jnp
from jax import lax
from jax.experimental import pallas as pl
from jax.experimental.pallas import tpu as pltpu
from jax.sharding import PartitionSpec as P

AXES = ("blk", "shard")
SIDE = 4
LANES = 128


def place_of(device):
    blk, shard = divmod(device, 32)
    return {"x": (shard & 1) * 2 + (blk >> 1), "y": (shard >> 1) & 3, "z": shard >> 3, "c": blk & 1}


def device_at(x, y, z, c):
    return ((x & 1) * 2 + c) * 32 + z * 8 + y * 2 + (x >> 1)


def along(axis0, axis1, by):
    pairs = []
    for device in range(128):
        place = place_of(device)
        axis = axis1 if place["c"] else axis0
        place[axis] = (place[axis] + by) % SIDE
        pairs.append((device, device_at(**place)))
    return pairs


def to_core(value):
    pairs = []
    for device in range(128):
        place = place_of(device)
        place["c"] = 1 - place["c"]
        pairs.append((device, device_at(**place)))
    return lax.ppermute(value, AXES, pairs)


def shift(value, axes, by):
    return lax.ppermute(value, AXES, along(*axes, by))


COST = 4
SLOTS = 3
CALLS = ((0,), (4,), (1, 2), (5, 6), (3,), (7,))
ORDERS = (("x", "y"), ("y", "z"), ("z", "x"))


def spread(value, axes, here):
    out = jnp.zeros((SIDE,) + value.shape, value.dtype)
    out = lax.dynamic_update_index_in_dim(out, value, here, 0)
    for by in (2, 1, -1):
        got = shift(value, axes, by)
        out = lax.dynamic_update_index_in_dim(out, got, (here - by) % SIDE, 0)
    return out.reshape((SIDE * value.shape[0],) + value.shape[1:])


def in_vmem(value):
    return pltpu.with_memory_space_constraint(value, pltpu.VMEM)


def score_kernel(scale, halves, *refs):
    rows = refs[:halves]
    cent_ref, bias_ref, score_ref, stat_ref, staged, sems = refs[halves:]
    half = rows[0].shape[0]
    tiles = half // LANES
    lane = lax.broadcasted_iota(jnp.int32, (LANES, LANES), 1)
    copies = []
    for h in range(halves):
        score = (
            lax.dot_general(
                rows[h][...],
                cent_ref[...],
                (((1,), (1,)), ((), ())),
                preferred_element_type=jnp.float32,
            )
            * scale
            - bias_ref[...]
        )
        if h >= 2:
            copies[h - 2].wait()
        staged[h % 2] = score
        copy = pltpu.make_async_copy(
            staged.at[h % 2], score_ref.at[h // 2, pl.ds(h % 2 * half, half)], sems.at[h % 2]
        )
        copy.start()
        copies.append(copy)
        for t in range(tiles):
            part = score[t * LANES : (t + 1) * LANES]
            top = jnp.max(part, axis=1, keepdims=True)
            total = jnp.sum(jnp.exp(part - top), axis=1, keepdims=True)
            flat = jnp.where(lane == 0, top, total).T
            row = h % 2 * tiles + t
            stat_ref[h // 2, row : row + 1, :] = flat[0:1, :]
            stat_ref[h // 2, 2 * tiles + row : 2 * tiles + row + 1, :] = flat[1:2, :]
    for copy in copies[-2:]:
        copy.wait()


def score_blocks(pieces, centroids, bias, scale):
    rows = [h for piece in pieces for h in piece]
    half, width = rows[0].shape
    cent = centroids.shape[0]
    vmem = pl.BlockSpec(memory_space=pltpu.VMEM)
    count = half * len(rows)
    return pl.pallas_call(
        functools.partial(score_kernel, scale, len(rows)),
        out_shape=(
            jax.ShapeDtypeStruct((len(pieces), 2 * half, cent), jnp.float32),
            jax.ShapeDtypeStruct((len(pieces), 4 * half // LANES, LANES), jnp.float32),
        ),
        in_specs=[vmem] * (len(rows) + 2),
        out_specs=(pl.BlockSpec(memory_space=pl.ANY), vmem),
        scratch_shapes=[
            pltpu.VMEM((2, half, cent), jnp.float32),
            pltpu.SemaphoreType.DMA((2,)),
        ],
        compiler_params=pltpu.CompilerParams(vmem_limit_bytes=8 * 2**20),
        cost_estimate=pl.CostEstimate(
            flops=COST * 2 * count * width * cent,
            bytes_accessed=2 * width * (count + cent) + 4 * count * cent,
            transcendentals=count * cent,
        ),
        name="scores",
    )(*[in_vmem(r) for r in rows], in_vmem(centroids), in_vmem(bias))


def weight_kernel(calls, pieces, total_cent, total_rows, where_ref, stat_a, stat_b, *refs):
    score_refs = refs[: len(calls)]
    block_refs = refs[len(calls) : len(calls) + 2 * pieces]
    out_ref, sums_ref, loads_ref = refs[len(calls) + 2 * pieces : len(calls) + 2 * pieces + 3]
    scores, blocks, staged, rounded, lse, sems, score_sems, block_sems = refs[
        len(calls) + 2 * pieces + 3 :
    ]
    tiles = stat_a.shape[1] // 2
    half = block_refs[0].shape[0]
    from_call = [(c, k) for c, n in enumerate(calls) for k in range(n)]

    def score_copy(i, h):
        call, k = from_call[i]
        part = pl.ds(h * half, half)
        return pltpu.make_async_copy(
            score_refs[call].at[k, part], scores.at[i, part], score_sems.at[i, h]
        )

    def block_copy(i, h):
        return pltpu.make_async_copy(
            block_refs[2 * i + h], blocks.at[i, pl.ds(h * half, half)], block_sems.at[i, h]
        )

    for i in range(pieces):
        for h in range(2):
            score_copy(i, h).start()
        for h in range(2):
            block_copy(i, h).start()

    top = jnp.maximum(stat_a[:, :tiles, :], stat_b[:, :tiles, :])
    total = stat_a[:, tiles:, :] * jnp.exp(stat_a[:, :tiles, :] - top) + stat_b[
        :, tiles:, :
    ] * jnp.exp(stat_b[:, :tiles, :] - top)
    lse[...] = top + jnp.log(total)

    def copies(i, kind):
        slot = i % SLOTS
        here = where_ref[pieces + i]
        if kind == 0:
            return [
                pltpu.make_async_copy(
                    staged.at[slot].reshape(4, 2, 2, 2, 16, 512).at[:, :, x_lo, j],
                    out_ref.at[x_lo, 0, j, here],
                    sems.at[slot],
                )
                for x_lo in range(2)
                for j in range(2)
            ]
        return [
            pltpu.make_async_copy(
                staged.at[slot].reshape(4, 4, 2, 16, 512).at[:, :, j],
                out_ref.at[lax.rem(here, 2), 1, j, :, :, lax.div(here, 2)],
                sems.at[slot],
            )
            for j in range(2)
        ]

    def on_kind(i, act):
        for k in range(2):

            @pl.when(where_ref[i] == k)
            def _(k=k):
                for copy in copies(i, k):
                    act(copy)

    def add_sums(i):
        for h in range(2):
            block_copy(i, h).wait()
        part_sums = lax.dot_general(
            rounded[i % 2],
            blocks[i],
            (((0,), (0,)), ((), ())),
            preferred_element_type=jnp.float32,
        )
        if i == 0:
            sums_ref[...] = part_sums
        elif i + 1 < pieces:
            sums_ref[...] += part_sums
        else:
            sums_ref[...] = (sums_ref[...] + part_sums) * (1.0 / math.sqrt(total_rows))

    load = jnp.zeros((8, loads_ref.shape[1]), jnp.float32)
    for i in range(pieces):
        slot = i % SLOTS
        if i >= SLOTS:
            on_kind(i - SLOTS, lambda c: c.wait())
        for h in range(2):
            score_copy(i, h).wait()
        norm = lse[where_ref[i] * SIDE + where_ref[pieces + i]]
        for t in range(tiles):
            part = pl.ds(t * LANES, LANES)
            column = jnp.broadcast_to(norm[t : t + 1, :], (LANES, LANES)).T
            column = jnp.concatenate([column] * (scores.shape[2] // LANES), axis=1)
            weight = total_cent * jnp.exp(scores[i, part, :] - column)
            staged[slot, part, :] = weight
            load = load + jnp.sum(weight.reshape(LANES // 8, 8, weight.shape[1]), axis=0)
            rounded[i % 2, part, :] = weight.astype(jnp.bfloat16)
        if i:
            add_sums(i - 1)
        on_kind(i, lambda c: c.start())
    add_sums(pieces - 1)
    loads_ref[...] = jnp.sum(load, axis=0, keepdims=True) * (1.0 / total_rows)
    for i in range(pieces - SLOTS, pieces):
        on_kind(i, lambda c: c.wait())


def weight_all(where, stat_a, stat_b, scores, blocks, total_cent, total_rows):
    calls = [score.shape[0] for score in scores]
    pieces = sum(calls)
    _, count, cent = scores[0].shape
    width = blocks[0].shape[1]
    vmem = pl.BlockSpec(memory_space=pltpu.VMEM)
    hbm = pl.BlockSpec(memory_space=pl.ANY)
    return pl.pallas_call(
        functools.partial(weight_kernel, calls, pieces, float(total_cent), float(total_rows)),
        out_shape=(
            jax.ShapeDtypeStruct((2, 2, 2, 4, 4, 2, 16, cent), jnp.float32),
            jax.ShapeDtypeStruct((cent, width), jnp.float32),
            jax.ShapeDtypeStruct((1, cent), jnp.float32),
        ),
        in_specs=[pl.BlockSpec(memory_space=pltpu.SMEM), vmem, vmem]
        + [hbm] * (len(scores) + len(blocks)),
        out_specs=(hbm, vmem, vmem),
        scratch_shapes=[
            pltpu.VMEM((pieces, count, cent), jnp.float32),
            pltpu.VMEM((pieces, count, width), jnp.bfloat16),
            pltpu.VMEM((SLOTS, count, cent), jnp.float32),
            pltpu.VMEM((2, count, cent), jnp.bfloat16),
            pltpu.VMEM((stat_a.shape[0], stat_a.shape[1] // 2, LANES), jnp.float32),
            pltpu.SemaphoreType.DMA((SLOTS,)),
            pltpu.SemaphoreType.DMA((pieces, 2)),
            pltpu.SemaphoreType.DMA((pieces, 2)),
        ],
        compiler_params=pltpu.CompilerParams(vmem_limit_bytes=30 * 2**20),
        name="weights",
    )(
        where,
        stat_a,
        stat_b,
        *[pltpu.with_memory_space_constraint(v, pltpu.HBM) for v in (*scores, *blocks)],
    )


def merged(stats):
    half = stats[0].shape[1] // 2
    tops = [s[:, :half] for s in stats]
    top = functools.reduce(jnp.maximum, tops)
    total = sum(s[:, half:] * jnp.exp(t - top) for s, t in zip(stats, tops))
    return jnp.concatenate([top, total], axis=1)


def per_device(embeddings, centroids, prices):
    blk, shard = lax.axis_index("blk"), lax.axis_index("shard")
    core = blk % 2
    at = {"x": (shard % 2) * 2 + blk // 2, "y": (shard // 2) % 4, "z": shard // 8}
    here = [jnp.where(core == 0, at[a], at[b]) for a, b in ORDERS]
    width = embeddings.shape[2]
    cent = centroids.shape[0]
    scale = 1.0 / math.sqrt(width)
    bias = (prices.astype(jnp.float32) / 1024.0).reshape(1, cent)
    total_cent = cent * 128
    total_rows = embeddings.shape[0] * embeddings.shape[1] * 128

    block = embeddings.reshape(-1, width)
    block = spread(block, ORDERS[0], here[0])
    block = spread(block, ORDERS[1], here[1])
    half = block.shape[0] // 2
    axes = ORDERS[2]
    own_a, own_b = block[:half], block[half:]
    before_a, before_b = shift(own_a, axes, 1), shift(own_b, axes, 1)
    after_b, after_a = shift(own_b, axes, -1), shift(own_a, axes, -1)
    across_a, across_b = shift(before_a, axes, 1), shift(after_b, axes, -1)
    steps = (0, 1, -1, 2)
    mine = [(own_a, own_b), (before_a, before_b), (after_a, after_b), (across_a, across_b)]
    their_own = to_core(block)
    theirs = [(their_own[:half], their_own[half:])]
    theirs += [tuple(to_core(h) for h in piece) for piece in mine[1:]]
    blocks = mine + theirs
    other = jnp.where(core == 0, at["x"], at["z"])
    last = [(here[2] - by) % SIDE for by in steps] + [(other - by) % SIDE for by in steps]

    stats = jnp.zeros((2 * SIDE, 8, LANES), jnp.float32)
    scores, order = [], []
    for call in CALLS:
        score, stat = score_blocks([blocks[i] for i in call], centroids, bias, scale)
        scores.append(score)
        order += call
        for k, i in enumerate(call):
            kind = core if i < SIDE else 1 - core
            stats = lax.dynamic_update_index_in_dim(stats, stat[k], kind * SIDE + last[i], 0)
    for axes in ORDERS:
        stats = merged([stats] + [shift(stats, axes, by) for by in (2, 1, -1)])
    kinds = [core if i < SIDE else 1 - core for i in order]
    where = jnp.stack(kinds + [last[i] for i in order]).astype(jnp.int32)
    out, sums, loads = weight_all(
        where,
        stats,
        to_core(stats),
        scores,
        [h for i in order for h in blocks[i]],
        total_cent,
        total_rows,
    )
    return out.reshape(8, 512, cent), sums, loads.reshape(cent)


def solution(mesh):
    placed = (P("blk", "shard", None), P(AXES, None), P(AXES))
    return jax.shard_map(
        per_device,
        mesh=mesh,
        in_specs=placed,
        out_specs=(P(None, None, AXES), P(AXES, None), P(AXES)),
        check_vma=False,
    )
```

```python
import functools
import math

import jax
import jax.numpy as jnp
from jax import lax
from jax.experimental import pallas as pl
from jax.experimental.pallas import tpu as pltpu
from jax.sharding import PartitionSpec as P

AXES = ("blk", "shard")
SIDE = 4
LANES = 128
CHUNK = 256


def place_of(device):
    blk, shard = divmod(device, 32)
    return {"x": (shard & 1) * 2 + (blk >> 1), "y": (shard >> 1) & 3, "z": shard >> 3, "c": blk & 1}


def device_at(x, y, z, c):
    return ((x & 1) * 2 + c) * 32 + z * 8 + y * 2 + (x >> 1)


def along(axis0, axis1, by):
    pairs = []
    for device in range(128):
        place = place_of(device)
        axis = axis1 if place["c"] else axis0
        place[axis] = (place[axis] + by) % SIDE
        pairs.append((device, device_at(**place)))
    return pairs


def to_core(value):
    pairs = []
    for device in range(128):
        place = place_of(device)
        place["c"] = 1 - place["c"]
        pairs.append((device, device_at(**place)))
    return lax.ppermute(value, AXES, pairs)


def shift(value, axes, by):
    return lax.ppermute(value, AXES, along(*axes, by))


COST = 1
SWAPS = ((), (0, 1), (2,))
SLOTS = 3
STEPS = (0, 1, -1, 2)
TURN = (0, 1, 3, 2)
ORDERS = (("x", "z"), ("y", "x"), ("z", "y"))


def spread(value, axes, here):
    out = jnp.zeros((SIDE,) + value.shape, value.dtype)
    out = lax.dynamic_update_index_in_dim(out, value, here, 0)
    for by in (2, 1, -1):
        got = shift(value, axes, by)
        out = lax.dynamic_update_index_in_dim(out, got, (here - by) % SIDE, 0)
    return out.reshape((SIDE * value.shape[0],) + value.shape[1:])


def places():
    blk, shard = lax.axis_index("blk"), lax.axis_index("shard")
    at = {"x": (shard & 1) * 2 + (blk >> 1), "y": (shard >> 1) & 3, "z": shard >> 3}
    return blk & 1, [[at[axes[kind]] for axes in ORDERS] for kind in range(2)]


def sources(place):
    return [(place[2] - by) & 3 for by in STEPS], [(place[1] + by) & 3 for by in TURN]


def in_vmem(value):
    return pltpu.with_memory_space_constraint(value, pltpu.VMEM)


def in_hbm(value):
    return pltpu.with_memory_space_constraint(value, pltpu.HBM)


def score_kernel(scale, sizes, *refs):
    count = sum(len(parts) for parts in sizes)
    rows = refs[:count]
    cents, biases = refs[count : count + 2], refs[count + 2 : count + 4]
    outs, refs = refs[count + 4 : count + 6], refs[count + 6 :]
    stat_ref, staged, part_sems, kept_sems = refs
    cent, width = cents[0].shape
    core, place = places()
    mids = [sources(p)[1] for p in place]
    mid = [jnp.where(core == 0, a, b) for a, b in zip(*mids)]
    lane = lax.broadcasted_iota(jnp.int32, (LANES, LANES), 1)
    copies = []
    ref = iter(rows)
    for k, parts in enumerate(sizes):
        done = 0
        for n, size in enumerate(parts):
            rows_ref = next(ref)
            copy = pltpu.make_async_copy(
                rows_ref, outs[1].at[k, pl.ds(done, size), pl.ds(cent, width)], kept_sems.at[k, n]
            )
            copy.start()
            copies.append(copy)
            done += size
    ref = iter(rows)
    for k, parts in enumerate(sizes):
        done = 0
        for size in parts:
            rows_ref = next(ref)
            for start in range(0, size, CHUNK):
                scores = [
                    lax.dot_general(
                        rows_ref[start : start + CHUNK, :],
                        cent_ref[...],
                        (((1,), (1,)), ((), ())),
                        preferred_element_type=jnp.float32,
                    )
                    * scale
                    - bias_ref[...]
                    for cent_ref, bias_ref in zip(cents, biases)
                ]
                for t in range(CHUNK // LANES):
                    cut = slice(t * LANES, (t + 1) * LANES)
                    top = jnp.max(jnp.maximum(scores[0][cut], scores[1][cut]), axis=1, keepdims=True)
                    powers = [jnp.exp(score[cut] - top) for score in scores]
                    for c, power in enumerate(powers):
                        staged[c, k, done : done + LANES, :] = power.astype(jnp.bfloat16)
                    total = jnp.sum(powers[0] + powers[1], axis=1, keepdims=True)
                    flat = jnp.where(lane == 0, top, total).T
                    row = mid[done // LANES]
                    stat_ref[k, pl.ds(row, 1), :] = flat[0:1, :]
                    stat_ref[k, pl.ds(SIDE + row, 1), :] = flat[1:2, :]
                    done += LANES
                half = done - CHUNK
                for c in range(2):
                    copy = pltpu.make_async_copy(
                        staged.at[c, k, pl.ds(half, CHUNK)],
                        outs[c].at[k, pl.ds(half, CHUNK), pl.ds(0, cent)],
                        part_sems.at[c, k, half // CHUNK],
                    )
                    copy.start()
                    copies.append(copy)
    for copy in copies:
        copy.wait()


def score_blocks(pieces, cents, biases, scale):
    sizes = [[rows.shape[0] for rows in piece] for piece in pieces]
    rows = [r for piece in pieces for r in piece]
    width = rows[0].shape[1]
    cent = cents[0].shape[0]
    height = sum(sizes[0])
    n = len(pieces)
    count = height * n
    hbm = pl.BlockSpec(memory_space=pl.ANY)
    vmem = pl.BlockSpec(memory_space=pltpu.VMEM)
    return pl.pallas_call(
        functools.partial(score_kernel, scale, sizes),
        out_shape=(
            pltpu.HBM((n, height, cent), jnp.bfloat16),
            pltpu.HBM((n, height, cent + width), jnp.bfloat16),
            jax.ShapeDtypeStruct((n, 2 * height // LANES, LANES), jnp.float32),
        ),
        in_specs=[vmem] * (len(rows) + 4),
        out_specs=(hbm, hbm, vmem),
        scratch_shapes=[
            pltpu.VMEM((2, n, height, cent), jnp.bfloat16),
            pltpu.SemaphoreType.DMA((2, n, height // CHUNK)),
            pltpu.SemaphoreType.DMA((n, 2)),
        ],
        compiler_params=pltpu.CompilerParams(vmem_limit_bytes=14 * 2**20),
        cost_estimate=pl.CostEstimate(
            flops=int(COST * 4 * count * width * cent),
            bytes_accessed=int(COST * (2 * width * (count + 2 * cent) + 4 * count * cent)),
            transcendentals=int(COST * 2 * count * cent),
        ),
        name="scores",
    )(*[in_vmem(v) for v in (*rows, *cents, *biases)])


def weight_kernel(spots, total_rows, *refs):
    pieces = 2 * SIDE
    calls = 1 + max(call for call, _ in spots)
    factors, refs = refs[:2], refs[2:]
    ours, sent, got, refs = refs[:calls], refs[calls : 2 * calls], refs[2 * calls : 3 * calls], refs[3 * calls :]
    out_ref, sums_ref, loads_ref, parts, blocks, staged, rounded, sems, part_sems, block_sems = refs
    tiles = SIDE
    cent = sums_ref.shape[0]

    def fetches(i):
        if i >= SIDE:
            return ()
        call, k = spots[i]
        return (
            pltpu.make_async_copy(ours[call].at[k], parts.at[i], part_sems.at[i]),
            pltpu.make_async_copy(
                sent[call].at[k, :, pl.ds(cent, blocks.shape[2])], blocks.at[i], block_sems.at[i]
            ),
        )

    def part_of(i, part):
        if i < SIDE:
            return parts[i, part, :]
        call, k = spots[i - SIDE]
        return got[call][k, part, :cent]

    def block_of(i):
        if i < SIDE:
            return blocks[i]
        call, k = spots[i - SIDE]
        return got[call][k, :, cent:]

    for i in range(SIDE):
        for copy in fetches(i):
            copy.start()

    here, place = places()
    found = [sources(p) for p in place]

    def body(core):
        def sends(i):
            slot = i % SLOTS
            kind = core if i < SIDE else 1 - core
            last = found[kind][0][i % SIDE]
            for x_lo in range(2):
                for j in range(2):
                    if kind == 0:
                        there = out_ref.at[x_lo, 0, j, last]
                    else:
                        there = out_ref.at[x_lo, 1, j, :, last]
                    yield pltpu.make_async_copy(staged.at[slot, x_lo, j], there, sems.at[slot])

        def add_sums(i):
            for copy in fetches(i)[1:]:
                copy.wait()
            part_sums = lax.dot_general(
                rounded[i % 2],
                block_of(i),
                (((0,), (0,)), ((), ())),
                preferred_element_type=jnp.float32,
            )
            if i == 0:
                sums_ref[...] = part_sums
            elif i + 1 < pieces:
                sums_ref[...] += part_sums
            else:
                sums_ref[...] = (sums_ref[...] + part_sums) * (1.0 / math.sqrt(total_rows))

        load = jnp.zeros((8, cent), jnp.float32)
        for i in range(pieces):
            slot = i % SLOTS
            if i >= SLOTS:
                for copy in sends(i - SLOTS):
                    copy.wait()
            kind = core if i < SIDE else 1 - core
            for copy in fetches(i)[:1]:
                copy.wait()
            for t in range(tiles):
                mid = found[kind][1][t]
                part = slice(t * LANES, (t + 1) * LANES)
                row = factors[i // SIDE][found[kind][0][i % SIDE], pl.ds(mid, 1), :]
                column = jnp.broadcast_to(row, (LANES, LANES)).T
                column = jnp.concatenate([column] * (cent // LANES), axis=1)
                weight = part_of(i, part).astype(jnp.float32) * column
                for p in range(SIDE):
                    for j in range(2):
                        chunk = weight[(p * 2 + j) * 16 : (p * 2 + j) * 16 + 16]
                        if kind == 0:
                            staged[slot, p % 2, j, mid, p // 2] = chunk
                        else:
                            staged[slot, mid & 1, j, p, mid >> 1] = chunk
                load = load + jnp.sum(weight.reshape(LANES // 8, 8, cent), axis=0)
                rounded[i % 2, part, :] = weight.astype(jnp.bfloat16)
            if i:
                add_sums(i - 1)
            for copy in sends(i):
                copy.start()
        add_sums(pieces - 1)
        loads_ref[...] = jnp.sum(load, axis=0, keepdims=True) * (1.0 / total_rows)
        for i in range(pieces - SLOTS, pieces):
            for copy in sends(i):
                copy.wait()

    for core in range(2):

        @pl.when(here == core)
        def _(core=core):
            body(core)


def weight_all(factors, ours, sent, got, spots, total_rows):
    _, height, cent = ours[0].shape
    width = sent[0].shape[2] - cent
    vmem = pl.BlockSpec(memory_space=pltpu.VMEM)
    hbm = pl.BlockSpec(memory_space=pl.ANY)
    return pl.pallas_call(
        functools.partial(weight_kernel, spots, float(total_rows)),
        out_shape=(
            jax.ShapeDtypeStruct((2, 2, 2, 4, 4, 2, 16, cent), jnp.float32),
            jax.ShapeDtypeStruct((cent, width), jnp.float32),
            jax.ShapeDtypeStruct((1, cent), jnp.float32),
        ),
        in_specs=[vmem] * 2
        + [hbm] * (len(ours) + len(sent))
        + [vmem] * len(got),
        out_specs=(hbm, vmem, vmem),
        scratch_shapes=[
            pltpu.VMEM((SIDE, height, cent), jnp.bfloat16),
            pltpu.VMEM((SIDE, height, width), jnp.bfloat16),
            pltpu.VMEM((SLOTS, 2, 2, 4, 2, 16, cent), jnp.float32),
            pltpu.VMEM((2, height, cent), jnp.bfloat16),
            pltpu.SemaphoreType.DMA((SLOTS,)),
            pltpu.SemaphoreType.DMA((SIDE,)),
            pltpu.SemaphoreType.DMA((SIDE,)),
        ],
        compiler_params=pltpu.CompilerParams(vmem_limit_bytes=20 * 2**20),
        name="weights",
    )(*factors, *[in_hbm(v) for v in (*ours, *sent)], *[in_vmem(v) for v in got])


def merged(stats):
    half = stats[0].shape[1] // 2
    tops = [s[:, :half] for s in stats]
    top = functools.reduce(jnp.maximum, tops)
    total = sum(s[:, half:] * jnp.exp(t - top) for s, t in zip(stats, tops))
    return jnp.concatenate([top, total], axis=1)


def per_device(embeddings, centroids, prices):
    core, place = places()
    first_place = jnp.where(core == 0, place[0][0], place[1][0])
    lasts = [sources(p)[0] for p in place]
    width = embeddings.shape[2]
    cent = centroids.shape[0]
    scale = 1.0 / math.sqrt(width)
    bias = (prices.astype(jnp.float32) / 1024.0).reshape(1, cent)
    with jax.named_scope("core"):
        cents, biases = (centroids, to_core(centroids)), (bias, to_core(bias))
    total_cent = cent * 128
    total_rows = embeddings.shape[0] * embeddings.shape[1] * 128

    first = spread(embeddings.reshape(-1, width), ORDERS[0], first_place)
    with jax.named_scope("mid"):
        mids = [first] + [shift(first, ORDERS[1], -by if by < 3 else 1) for by in TURN[1:]]
    own = jnp.concatenate(mids)
    half = own.shape[0] // 2
    axes = ORDERS[2]
    lasts = [jnp.where(core == 0, a, b) for a, b in zip(*lasts)]
    local = jnp.zeros((SIDE, 8, LANES), jnp.float32)
    ours, theirs, got, spots = [], [], [], []

    def score(call, pieces, local):
        our, their, stat = score_blocks(pieces, cents, biases, scale)
        for k, i in enumerate(call):
            spots.append((len(ours), k))
            local = lax.dynamic_update_index_in_dim(local, stat[k], lasts[i], 0)
        ours.append(our)
        theirs.append(their)
        return local

    with jax.named_scope("last"):
        before, after = shift(own, axes, 1), shift(own, axes, -1)
    local = score((0,), [(own,)], local)
    before, after, local = lax.optimization_barrier((before, after, local))
    with jax.named_scope("across"):
        across = shift(before[:half], axes, 1), shift(after[half:], axes, -1)
    local = score((1, 2), [(before,), (after,)], local)
    *across, local = lax.optimization_barrier((*across, local))
    local = score((3,), [across], local)
    stats = local
    for axes, calls in zip(ORDERS, SWAPS):
        with jax.named_scope("core"):
            new = [to_core(theirs[c]) for c in calls]
        stats = merged([stats] + [shift(stats, axes, by) for by in (2, 1, -1)])
        stats, theirs, new = lax.optimization_barrier((stats, theirs, new))
        got += new
    factor = total_cent * jnp.exp(local[:, :SIDE] - (stats[:, :SIDE] + jnp.log(stats[:, SIDE:])))
    with jax.named_scope("core"):
        factors = factor, to_core(factor)
    out, sums, loads = weight_all(factors, ours, theirs, got, spots, total_rows)
    return out.reshape(8, 512, cent), sums, loads.reshape(cent)


def solution(mesh):
    placed = (P("blk", "shard", None), P(AXES, None), P(AXES))
    return jax.shard_map(
        per_device,
        mesh=mesh,
        in_specs=placed,
        out_specs=(P(None, None, AXES), P(AXES, None), P(AXES)),
        check_vma=False,
    )
```

```python
import functools
import math

import jax
import jax.numpy as jnp
from jax import lax
from jax.experimental import pallas as pl
from jax.experimental.pallas import tpu as pltpu
from jax.sharding import PartitionSpec as P

AXES = ("blk", "shard")
SIDE = 4
LANES = 128


def place_of(device):
    blk, shard = divmod(device, 32)
    return {"x": (shard & 1) * 2 + (blk >> 1), "y": (shard >> 1) & 3, "z": shard >> 3, "c": blk & 1}


def device_at(x, y, z, c):
    return ((x & 1) * 2 + c) * 32 + z * 8 + y * 2 + (x >> 1)


def along(axis0, axis1, by):
    pairs = []
    for device in range(128):
        place = place_of(device)
        axis = axis1 if place["c"] else axis0
        place[axis] = (place[axis] + by) % SIDE
        pairs.append((device, device_at(**place)))
    return pairs


def to_core(value):
    pairs = []
    for device in range(128):
        place = place_of(device)
        place["c"] = 1 - place["c"]
        pairs.append((device, device_at(**place)))
    return lax.ppermute(value, AXES, pairs)


def shift(value, axes, by):
    return lax.ppermute(value, AXES, along(*axes, by))


COST = 1
SWAPS = ((), (0, 1), (2, 3))
SLOTS = 3
SPLIT = 2
STEPS = (0, 1, -1, 2)
TURN = (0, 1, 3, 2)
ORDERS = (("x", "z"), ("y", "x"), ("z", "y"))


def spread(value, axes, here):
    out = jnp.zeros((SIDE,) + value.shape, value.dtype)
    out = lax.dynamic_update_index_in_dim(out, value, here, 0)
    for by in (2, 1, -1):
        got = shift(value, axes, by)
        out = lax.dynamic_update_index_in_dim(out, got, (here - by) % SIDE, 0)
    return out.reshape((SIDE * value.shape[0],) + value.shape[1:])


def places():
    blk, shard = lax.axis_index("blk"), lax.axis_index("shard")
    at = {"x": (shard & 1) * 2 + (blk >> 1), "y": (shard >> 1) & 3, "z": shard >> 3}
    return blk & 1, [[at[axes[kind]] for axes in ORDERS] for kind in range(2)]


def sources(place):
    return [(place[2] - by) & 3 for by in STEPS], [(place[1] + by) & 3 for by in TURN]


def in_vmem(value):
    return pltpu.with_memory_space_constraint(value, pltpu.VMEM)


def in_hbm(value):
    return pltpu.with_memory_space_constraint(value, pltpu.HBM)


def score_kernel(scale, units, rows_a, rows_b, cent_a, cent_b, bias_a, bias_b, before_ref, *refs):
    ours_ref, sent_ref, stat_ref, staged, part_sems, row_sems = refs
    cent, width = cent_a.shape
    size = rows_a.shape[0]
    core, place = places()
    lasts, mids = zip(*[sources(p) for p in place])
    lane = lax.broadcasted_iota(jnp.int32, (LANES, LANES), 1)
    copies = []
    for u, rows_ref in enumerate((rows_a, rows_b)):
        copy = pltpu.make_async_copy(
            rows_ref, sent_ref.at[u, :, pl.ds(cent, width)], row_sems.at[u]
        )
        copy.start()
        copies.append(copy)
    stat_ref[...] = before_ref[...]
    for u, rows_ref in enumerate((rows_a, rows_b)):
        piece, half = units[u]
        last = jnp.where(core == 0, lasts[0][piece], lasts[1][piece])
        scores = [
            lax.dot_general(
                rows_ref[...],
                cent_ref[...],
                (((1,), (1,)), ((), ())),
                preferred_element_type=jnp.float32,
            )
            * scale
            - bias_ref[...]
            for cent_ref, bias_ref in ((cent_a, bias_a), (cent_b, bias_b))
        ]
        for t in range(size // LANES):
            cut = slice(t * LANES, (t + 1) * LANES)
            top = jnp.max(jnp.maximum(scores[0][cut], scores[1][cut]), axis=1, keepdims=True)
            powers = [jnp.exp(score[cut] - top) for score in scores]
            for c, power in enumerate(powers):
                staged[c, u, cut, :] = power.astype(jnp.bfloat16)
            total = jnp.sum(powers[0] + powers[1], axis=1, keepdims=True)
            flat = jnp.where(lane == 0, top, total).T
            turn = half * (size // LANES) + t
            row = jnp.where(core == 0, mids[0][turn], mids[1][turn])
            stat_ref[last, pl.ds(row, 1), :] = flat[0:1, :]
            stat_ref[last, pl.ds(SIDE + row, 1), :] = flat[1:2, :]
        for c, there in enumerate((ours_ref.at[u], sent_ref.at[u, :, pl.ds(0, cent)])):
            copy = pltpu.make_async_copy(staged.at[c, u], there, part_sems.at[c, u])
            copy.start()
            copies.append(copy)
    for copy in copies:
        copy.wait()


def score_rows(units, rows, cents, biases, local, scale):
    size, width = rows[0].shape
    cent = cents[0].shape[0]
    hbm = pl.BlockSpec(memory_space=pl.ANY)
    vmem = pl.BlockSpec(memory_space=pltpu.VMEM)
    return pl.pallas_call(
        functools.partial(score_kernel, scale, units),
        out_shape=(
            pltpu.HBM((2, size, cent), jnp.bfloat16),
            pltpu.HBM((2, size, cent + width), jnp.bfloat16),
            jax.ShapeDtypeStruct(local.shape, jnp.float32),
        ),
        in_specs=[vmem] * 7,
        out_specs=(hbm, hbm, vmem),
        scratch_shapes=[
            pltpu.VMEM((2, 2, size, cent), jnp.bfloat16),
            pltpu.SemaphoreType.DMA((2, 2)),
            pltpu.SemaphoreType.DMA((2,)),
        ],
        compiler_params=pltpu.CompilerParams(vmem_limit_bytes=14 * 2**20),
        cost_estimate=pl.CostEstimate(
            flops=int(COST * 8 * size * width * cent),
            bytes_accessed=int(COST * (4 * width * (size + cent) + 8 * size * cent)),
            transcendentals=int(COST * 4 * size * cent),
        ),
        name="scores",
    )(*[in_vmem(v) for v in (*rows, *cents, *biases)], local)


def weight_kernel(spots, total_rows, *refs):
    pieces = 2 * SIDE
    calls = len(spots) // 2
    factors, refs = refs[:2], refs[2:]
    ours, sent, got, refs = refs[:calls], refs[calls : 2 * calls], refs[2 * calls : 3 * calls], refs[3 * calls :]
    out_ref, sums_ref, loads_ref, parts, blocks, staged, rounded, sems, part_sems, block_sems = refs
    tiles = SIDE
    cent = sums_ref.shape[0]
    half = parts.shape[1] // 2

    def fetches(i):
        if i >= SIDE:
            return ()
        moves = []
        for h in range(2):
            call, u = spots[2 * i + h]
            there = pl.ds(h * half, half)
            moves += [
                pltpu.make_async_copy(ours[call].at[u], parts.at[i, there], part_sems.at[i, h]),
                pltpu.make_async_copy(
                    sent[call].at[u, :, pl.ds(cent, blocks.shape[2])],
                    blocks.at[i, there],
                    block_sems.at[i, h],
                ),
            ]
        return moves

    def part_of(i, t):
        if i < SIDE:
            return parts[i, t * LANES : (t + 1) * LANES, :]
        call, u = spots[2 * (i - SIDE) + t * LANES // half]
        start = t * LANES % half
        return got[call][u, start : start + LANES, :cent]

    def block_of(i, cols):
        if i < SIDE:
            return blocks[i, :, cols]
        halves = [spots[2 * (i - SIDE) + h] for h in range(2)]
        there = slice(cent + cols.start, cent + cols.stop)
        return jnp.concatenate([got[call][u, :, there] for call, u in halves])

    for i in range(SIDE):
        for copy in fetches(i):
            copy.start()

    here, place = places()
    found = [sources(p) for p in place]

    def body(core):
        def sends(i):
            slot = i % SLOTS
            kind = core if i < SIDE else 1 - core
            last = found[kind][0][i % SIDE]
            for x_lo in range(2):
                for j in range(2):
                    if kind == 0:
                        there = out_ref.at[x_lo, 0, j, last]
                    else:
                        there = out_ref.at[x_lo, 1, j, :, last]
                    yield pltpu.make_async_copy(staged.at[slot, x_lo, j], there, sems.at[slot])

        def add_sums(i, part):
            width = blocks.shape[2] // SPLIT
            cols = slice(part * width, (part + 1) * width)
            part_sums = lax.dot_general(
                rounded[i % 2],
                block_of(i, cols),
                (((0,), (0,)), ((), ())),
                preferred_element_type=jnp.float32,
            )
            if i == 0:
                sums_ref[:, cols] = part_sums
            elif i + 1 < pieces:
                sums_ref[:, cols] += part_sums
            else:
                sums_ref[:, cols] = (sums_ref[:, cols] + part_sums) * (1.0 / math.sqrt(total_rows))

        def weigh(i, t):
            slot = i % SLOTS
            kind = core if i < SIDE else 1 - core
            mid = found[kind][1][t]
            part = slice(t * LANES, (t + 1) * LANES)
            row = factors[i // SIDE][found[kind][0][i % SIDE], pl.ds(mid, 1), :]
            column = jnp.broadcast_to(row, (LANES, LANES)).T
            column = jnp.concatenate([column] * (cent // LANES), axis=1)
            weight = part_of(i, t).astype(jnp.float32) * column
            for p in range(SIDE):
                for j in range(2):
                    chunk = weight[(p * 2 + j) * 16 : (p * 2 + j) * 16 + 16]
                    if kind == 0:
                        staged[slot, p % 2, j, mid, p // 2] = chunk
                    else:
                        staged[slot, mid & 1, j, p, mid >> 1] = chunk
            rounded[i % 2, part, :] = weight.astype(jnp.bfloat16)
            return jnp.sum(weight.reshape(LANES // 8, 8, cent), axis=0)

        load = jnp.zeros((8, cent), jnp.float32)
        for i in range(pieces):
            if i >= SLOTS:
                for copy in sends(i - SLOTS):
                    copy.wait()
            for copy in fetches(i):
                copy.wait()
            for t in range(tiles):
                load = load + weigh(i, t)
                if i and (t + 1) % (tiles // SPLIT) == 0:
                    add_sums(i - 1, t // (tiles // SPLIT))
            for copy in sends(i):
                copy.start()
        for part in range(SPLIT):
            add_sums(pieces - 1, part)
        loads_ref[...] = jnp.sum(load, axis=0, keepdims=True) * (1.0 / total_rows)
        for i in range(pieces - SLOTS, pieces):
            for copy in sends(i):
                copy.wait()

    for core in range(2):

        @pl.when(here == core)
        def _(core=core):
            body(core)


def weight_all(factors, ours, sent, got, spots, total_rows):
    _, size, cent = ours[0].shape
    height = 2 * size
    width = sent[0].shape[2] - cent
    vmem = pl.BlockSpec(memory_space=pltpu.VMEM)
    hbm = pl.BlockSpec(memory_space=pl.ANY)
    return pl.pallas_call(
        functools.partial(weight_kernel, spots, float(total_rows)),
        out_shape=(
            jax.ShapeDtypeStruct((2, 2, 2, 4, 4, 2, 16, cent), jnp.float32),
            jax.ShapeDtypeStruct((cent, width), jnp.float32),
            jax.ShapeDtypeStruct((1, cent), jnp.float32),
        ),
        in_specs=[vmem] * 2
        + [hbm] * (len(ours) + len(sent))
        + [vmem] * len(got),
        out_specs=(hbm, vmem, vmem),
        scratch_shapes=[
            pltpu.VMEM((SIDE, height, cent), jnp.bfloat16),
            pltpu.VMEM((SIDE, height, width), jnp.bfloat16),
            pltpu.VMEM((SLOTS, 2, 2, 4, 2, 16, cent), jnp.float32),
            pltpu.VMEM((2, height, cent), jnp.bfloat16),
            pltpu.SemaphoreType.DMA((SLOTS,)),
            pltpu.SemaphoreType.DMA((SIDE, 2)),
            pltpu.SemaphoreType.DMA((SIDE, 2)),
        ],
        compiler_params=pltpu.CompilerParams(vmem_limit_bytes=20 * 2**20),
        name="weights",
    )(*factors, *[in_hbm(v) for v in (*ours, *sent)], *[in_vmem(v) for v in got])


def merged(stats):
    half = stats[0].shape[1] // 2
    tops = [s[:, :half] for s in stats]
    top = functools.reduce(jnp.maximum, tops)
    total = sum(s[:, half:] * jnp.exp(t - top) for s, t in zip(stats, tops))
    return jnp.concatenate([top, total], axis=1)


def per_device(embeddings, centroids, prices):
    core, place = places()
    first_place = jnp.where(core == 0, place[0][0], place[1][0])
    width = embeddings.shape[2]
    cent = centroids.shape[0]
    scale = 1.0 / math.sqrt(width)
    bias = (prices.astype(jnp.float32) / 1024.0).reshape(1, cent)
    with jax.named_scope("core"):
        cents, biases = (centroids, to_core(centroids)), (bias, to_core(bias))
    total_cent = cent * 128
    total_rows = embeddings.shape[0] * embeddings.shape[1] * 128

    first = spread(embeddings.reshape(-1, width), ORDERS[0], first_place)
    first, cents, biases = lax.optimization_barrier((first, cents, biases))
    with jax.named_scope("mid"):
        mids = [first] + [shift(first, ORDERS[1], -by if by < 3 else 1) for by in TURN[1:]]
    own_a, own_b = jnp.concatenate(mids[:2]), jnp.concatenate(mids[2:])
    axes = ORDERS[2]
    local = jnp.zeros((SIDE, 2 * SIDE, LANES), jnp.float32)
    ours, theirs, got, spots = [], [], [], {}

    def score(units, rows, local):
        our, their, local = score_rows(units, rows, cents, biases, local, scale)
        for u, unit in enumerate(units):
            spots[unit] = len(ours), u
        ours.append(our)
        theirs.append(their)
        return local

    with jax.named_scope("last"):
        before_a, after_b = shift(own_a, axes, 1), shift(own_b, axes, -1)
        before_b, after_a = shift(own_b, axes, 1), shift(own_a, axes, -1)
    with jax.named_scope("across"):
        across_a, across_b = shift(before_a, axes, 1), shift(after_b, axes, -1)
    local = score(((0, 0), (0, 1)), (own_a, own_b), local)
    local = score(((1, 0), (2, 1)), (before_a, after_b), local)
    before_b, after_a, local = lax.optimization_barrier((before_b, after_a, local))
    local = score(((1, 1), (2, 0)), (before_b, after_a), local)
    across_a, across_b, local = lax.optimization_barrier((across_a, across_b, local))
    local = score(((3, 0), (3, 1)), (across_a, across_b), local)
    spots = [spots[i, h] for i in range(SIDE) for h in range(2)]
    stats = local
    for axes, calls in zip(ORDERS, SWAPS):
        with jax.named_scope("core"):
            new = [to_core(theirs[c]) for c in calls]
        stats = merged([stats] + [shift(stats, axes, by) for by in (2, 1, -1)])
        stats, theirs, new = lax.optimization_barrier((stats, theirs, new))
        got += new
    factor = total_cent * jnp.exp(local[:, :SIDE] - (stats[:, :SIDE] + jnp.log(stats[:, SIDE:])))
    with jax.named_scope("core"):
        factors = factor, to_core(factor)
    out, sums, loads = weight_all(factors, ours, theirs, got, spots, total_rows)
    return out.reshape(8, 512, cent), sums, loads.reshape(cent)


def solution(mesh):
    placed = (P("blk", "shard", None), P(AXES, None), P(AXES))
    return jax.shard_map(
        per_device,
        mesh=mesh,
        in_specs=placed,
        out_specs=(P(None, None, AXES), P(AXES, None), P(AXES)),
        check_vma=False,
    )
```

```python
import functools
import math

import jax
import jax.numpy as jnp
from jax import lax
from jax.experimental import pallas as pl
from jax.experimental.pallas import tpu as pltpu
from jax.sharding import PartitionSpec as P

AXES = ("blk", "shard")
SIDE = 4
LANES = 128


def place_of(device):
    blk, shard = divmod(device, 32)
    return {"x": (shard & 1) * 2 + (blk >> 1), "y": (shard >> 1) & 3, "z": shard >> 3, "c": blk & 1}


def device_at(x, y, z, c):
    return ((x & 1) * 2 + c) * 32 + z * 8 + y * 2 + (x >> 1)


def along(axis0, axis1, by):
    pairs = []
    for device in range(128):
        place = place_of(device)
        axis = axis1 if place["c"] else axis0
        place[axis] = (place[axis] + by) % SIDE
        pairs.append((device, device_at(**place)))
    return pairs


def to_core(value):
    pairs = []
    for device in range(128):
        place = place_of(device)
        place["c"] = 1 - place["c"]
        pairs.append((device, device_at(**place)))
    return lax.ppermute(value, AXES, pairs)


def shift(value, axes, by):
    return lax.ppermute(value, AXES, along(*axes, by))


COST = 1
SWAPS = ((), (0, 1), (2, 3))
SLOTS = 3
SPLIT = 2
STEPS = (0, 1, -1, 2)
TURN = (0, 1, 3, 2)
ORDERS = (("x", "z"), ("y", "x"), ("z", "y"))


def spread(value, axes, here):
    out = jnp.zeros((SIDE,) + value.shape, value.dtype)
    out = lax.dynamic_update_index_in_dim(out, value, here, 0)
    for by in (2, 1, -1):
        got = shift(value, axes, by)
        out = lax.dynamic_update_index_in_dim(out, got, (here - by) % SIDE, 0)
    return out.reshape((SIDE * value.shape[0],) + value.shape[1:])


def places():
    blk, shard = lax.axis_index("blk"), lax.axis_index("shard")
    at = {"x": (shard & 1) * 2 + (blk >> 1), "y": (shard >> 1) & 3, "z": shard >> 3}
    return blk & 1, [[at[axes[kind]] for axes in ORDERS] for kind in range(2)]


def sources(place):
    return [(place[2] - by) & 3 for by in STEPS], [(place[1] + by) & 3 for by in TURN]


def in_vmem(value):
    return pltpu.with_memory_space_constraint(value, pltpu.VMEM)


def in_hbm(value):
    return pltpu.with_memory_space_constraint(value, pltpu.HBM)


def score_kernel(scale, units, rows_a, rows_b, cent_a, cent_b, bias_a, bias_b, before_ref, *refs):
    ours_ref, sent_ref, stat_ref, staged, part_sems, row_sems = refs
    cent, width = cent_a.shape
    size = rows_a.shape[0]
    core, place = places()
    lasts, mids = zip(*[sources(p) for p in place])
    lane = lax.broadcasted_iota(jnp.int32, (LANES, LANES), 1)
    copies = []
    for u, rows_ref in enumerate((rows_a, rows_b)):
        copy = pltpu.make_async_copy(
            rows_ref, sent_ref.at[u, :, pl.ds(cent, width)], row_sems.at[u]
        )
        copy.start()
        copies.append(copy)
    stat_ref[...] = before_ref[...]
    for u, rows_ref in enumerate((rows_a, rows_b)):
        piece, half = units[u]
        last = jnp.where(core == 0, lasts[0][piece], lasts[1][piece])
        scores = [
            lax.dot_general(
                rows_ref[...],
                cent_ref[...],
                (((1,), (1,)), ((), ())),
                preferred_element_type=jnp.float32,
            )
            * scale
            - bias_ref[...]
            for cent_ref, bias_ref in ((cent_a, bias_a), (cent_b, bias_b))
        ]
        for t in range(size // LANES):
            cut = slice(t * LANES, (t + 1) * LANES)
            top = jnp.max(jnp.maximum(scores[0][cut], scores[1][cut]), axis=1, keepdims=True)
            powers = [jnp.exp(score[cut] - top) for score in scores]
            staged[u, cut, :] = powers[0].astype(jnp.bfloat16)
            copy = pltpu.make_async_copy(
                staged.at[u, pl.ds(t * LANES, LANES)],
                ours_ref.at[u, pl.ds(t * LANES, LANES)],
                part_sems.at[u, t],
            )
            copy.start()
            copies.append(copy)
            sent_ref[u, cut, :cent] = powers[1].astype(jnp.bfloat16)
            total = jnp.sum(powers[0] + powers[1], axis=1, keepdims=True)
            flat = jnp.where(lane == 0, top, total).T
            turn = half * (size // LANES) + t
            row = jnp.where(core == 0, mids[0][turn], mids[1][turn])
            stat_ref[last, pl.ds(row, 1), :] = flat[0:1, :]
            stat_ref[last, pl.ds(SIDE + row, 1), :] = flat[1:2, :]
    for copy in copies:
        copy.wait()


def score_rows(units, rows, cents, biases, local, scale):
    size, width = rows[0].shape
    cent = cents[0].shape[0]
    vmem = pl.BlockSpec(memory_space=pltpu.VMEM)
    return pl.pallas_call(
        functools.partial(score_kernel, scale, units),
        out_shape=(
            pltpu.HBM((2, size, cent), jnp.bfloat16),
            pltpu.VMEM((2, size, cent + width), jnp.bfloat16),
            jax.ShapeDtypeStruct(local.shape, jnp.float32),
        ),
        in_specs=[vmem] * 7,
        out_specs=(pl.BlockSpec(memory_space=pl.ANY), vmem, vmem),
        scratch_shapes=[
            pltpu.VMEM((2, size, cent), jnp.bfloat16),
            pltpu.SemaphoreType.DMA((2, size // LANES)),
            pltpu.SemaphoreType.DMA((2,)),
        ],
        compiler_params=pltpu.CompilerParams(vmem_limit_bytes=14 * 2**20),
        cost_estimate=pl.CostEstimate(
            flops=int(COST * 8 * size * width * cent),
            bytes_accessed=int(COST * (4 * width * (size + cent) + 8 * size * cent)),
            transcendentals=int(COST * 4 * size * cent),
        ),
        name="scores",
    )(*[in_vmem(v) for v in (*rows, *cents, *biases)], local)


def weight_kernel(spots, total_rows, *refs):
    pieces = 2 * SIDE
    calls = len(spots) // 2
    factors, refs = refs[:2], refs[2:]
    ours, sent, got, refs = refs[:calls], refs[calls : 2 * calls], refs[2 * calls : 3 * calls], refs[3 * calls :]
    out_ref, sums_ref, loads_ref, *refs = refs
    parts, blocks, staged, rounded, sums, sems, part_sems, block_sems, sum_sems = refs
    order = [*range(SIDE, pieces), *range(SIDE)]
    tiles = SIDE
    cent = sums_ref.shape[0]
    half = parts.shape[1] // 2

    def fetches(i):
        if i >= SIDE:
            return ()
        moves = []
        for h in range(2):
            call, u = spots[2 * i + h]
            there = pl.ds(h * half, half)
            moves += [
                pltpu.make_async_copy(ours[call].at[u], parts.at[i, there], part_sems.at[i, h]),
                pltpu.make_async_copy(
                    sent[call].at[u, :, pl.ds(cent, blocks.shape[2])],
                    blocks.at[i, there],
                    block_sems.at[i, h],
                ),
            ]
        return moves

    def part_of(i, t):
        if i < SIDE:
            return parts[i, t * LANES : (t + 1) * LANES, :]
        call, u = spots[2 * (i - SIDE) + t * LANES // half]
        start = t * LANES % half
        return got[call][u, start : start + LANES, :cent]

    def block_of(i, cols):
        if i < SIDE:
            return blocks[i, :, cols]
        halves = [spots[2 * (i - SIDE) + h] for h in range(2)]
        there = slice(cent + cols.start, cent + cols.stop)
        return jnp.concatenate([got[call][u, :, there] for call, u in halves])

    for i in range(SIDE):
        for copy in fetches(i):
            copy.start()

    here, place = places()
    found = [sources(p) for p in place]

    def body(core):
        def sends(n):
            i, slot = order[n], n % SLOTS
            kind = core if i < SIDE else 1 - core
            last = found[kind][0][i % SIDE]
            for x_lo in range(2):
                for j in range(2):
                    if kind == 0:
                        there = out_ref.at[x_lo, 0, j, last]
                    else:
                        there = out_ref.at[x_lo, 1, j, :, last]
                    yield pltpu.make_async_copy(staged.at[slot, x_lo, j], there, sems.at[slot])

        def sum_copy(part):
            width = blocks.shape[2] // SPLIT
            cols = pl.ds(part * width, width)
            return pltpu.make_async_copy(sums.at[:, cols], sums_ref.at[:, cols], sum_sems.at[part])

        def add_sums(n, part):
            i = order[n]
            width = blocks.shape[2] // SPLIT
            cols = slice(part * width, (part + 1) * width)
            part_sums = lax.dot_general(
                rounded[n % 2],
                block_of(i, cols),
                (((0,), (0,)), ((), ())),
                preferred_element_type=jnp.float32,
            )
            if n == 0:
                sums[:, cols] = part_sums
            elif n + 1 < pieces:
                sums[:, cols] += part_sums
            else:
                sums[:, cols] = (sums[:, cols] + part_sums) * (1.0 / math.sqrt(total_rows))

        def weigh(n, t):
            i, slot = order[n], n % SLOTS
            kind = core if i < SIDE else 1 - core
            mid = found[kind][1][t]
            part = slice(t * LANES, (t + 1) * LANES)
            row = factors[i // SIDE][found[kind][0][i % SIDE], pl.ds(mid, 1), :]
            column = jnp.broadcast_to(row, (LANES, LANES)).T
            column = jnp.concatenate([column] * (cent // LANES), axis=1)
            weight = part_of(i, t).astype(jnp.float32) * column
            for p in range(SIDE):
                for j in range(2):
                    chunk = weight[(p * 2 + j) * 16 : (p * 2 + j) * 16 + 16]
                    if kind == 0:
                        staged[slot, p % 2, j, mid, p // 2] = chunk
                    else:
                        staged[slot, mid & 1, j, p, mid >> 1] = chunk
            rounded[n % 2, part, :] = weight.astype(jnp.bfloat16)
            return jnp.sum(weight.reshape(LANES // 8, 8, cent), axis=0)

        load = jnp.zeros((8, cent), jnp.float32)
        for n in range(pieces):
            if n >= SLOTS:
                for copy in sends(n - SLOTS):
                    copy.wait()
            for copy in fetches(order[n]):
                copy.wait()
            for t in range(tiles):
                load = load + weigh(n, t)
                if n and (t + 1) % (tiles // SPLIT) == 0:
                    add_sums(n - 1, t // (tiles // SPLIT))
            for copy in sends(n):
                copy.start()
        for part in range(SPLIT):
            add_sums(pieces - 1, part)
            sum_copy(part).start()
        loads_ref[...] = jnp.sum(load, axis=0, keepdims=True) * (1.0 / total_rows)
        for n in range(pieces - SLOTS, pieces):
            for copy in sends(n):
                copy.wait()
        for part in range(SPLIT):
            sum_copy(part).wait()

    for core in range(2):

        @pl.when(here == core)
        def _(core=core):
            body(core)


def weight_all(factors, ours, sent, got, spots, total_rows):
    _, size, cent = ours[0].shape
    height = 2 * size
    width = sent[0].shape[2] - cent
    vmem = pl.BlockSpec(memory_space=pltpu.VMEM)
    hbm = pl.BlockSpec(memory_space=pl.ANY)
    return pl.pallas_call(
        functools.partial(weight_kernel, spots, float(total_rows)),
        out_shape=(
            jax.ShapeDtypeStruct((2, 2, 2, 4, 4, 2, 16, cent), jnp.float32),
            jax.ShapeDtypeStruct((cent, width), jnp.float32),
            jax.ShapeDtypeStruct((1, cent), jnp.float32),
        ),
        in_specs=[vmem] * 2
        + [hbm] * (len(ours) + len(sent))
        + [vmem] * len(got),
        out_specs=(hbm, hbm, vmem),
        scratch_shapes=[
            pltpu.VMEM((SIDE, height, cent), jnp.bfloat16),
            pltpu.VMEM((SIDE, height, width), jnp.bfloat16),
            pltpu.VMEM((SLOTS, 2, 2, 4, 2, 16, cent), jnp.float32),
            pltpu.VMEM((2, height, cent), jnp.bfloat16),
            pltpu.VMEM((cent, width), jnp.float32),
            pltpu.SemaphoreType.DMA((SLOTS,)),
            pltpu.SemaphoreType.DMA((SIDE, 2)),
            pltpu.SemaphoreType.DMA((SIDE, 2)),
            pltpu.SemaphoreType.DMA((SPLIT,)),
        ],
        compiler_params=pltpu.CompilerParams(vmem_limit_bytes=20 * 2**20),
        name="weights",
    )(*factors, *[in_hbm(v) for v in (*ours, *sent)], *[in_vmem(v) for v in got])


def merged(stats):
    half = stats[0].shape[1] // 2
    tops = [s[:, :half] for s in stats]
    top = functools.reduce(jnp.maximum, tops)
    total = sum(s[:, half:] * jnp.exp(t - top) for s, t in zip(stats, tops))
    return jnp.concatenate([top, total], axis=1)


def per_device(embeddings, centroids, prices):
    core, place = places()
    first_place = jnp.where(core == 0, place[0][0], place[1][0])
    width = embeddings.shape[2]
    cent = centroids.shape[0]
    scale = 1.0 / math.sqrt(width)
    bias = (prices.astype(jnp.float32) / 1024.0).reshape(1, cent)
    with jax.named_scope("core"):
        cents, biases = (centroids, to_core(centroids)), (bias, to_core(bias))
    total_cent = cent * 128
    total_rows = embeddings.shape[0] * embeddings.shape[1] * 128

    first = spread(embeddings.reshape(-1, width), ORDERS[0], first_place)
    first, cents, biases = lax.optimization_barrier((first, cents, biases))
    with jax.named_scope("mid"):
        mids = [first] + [shift(first, ORDERS[1], -by if by < 3 else 1) for by in TURN[1:]]
    own_a, own_b = jnp.concatenate(mids[:2]), jnp.concatenate(mids[2:])
    axes = ORDERS[2]
    local = jnp.zeros((SIDE, 2 * SIDE, LANES), jnp.float32)
    ours, theirs, got, spots = [], [], [], {}

    def score(units, rows, local):
        our, their, local = score_rows(units, rows, cents, biases, local, scale)
        for u, unit in enumerate(units):
            spots[unit] = len(ours), u
        ours.append(our)
        theirs.append(their)
        return local

    with jax.named_scope("last"):
        before_a, after_b = shift(own_a, axes, 1), shift(own_b, axes, -1)
        before_b, after_a = shift(own_b, axes, 1), shift(own_a, axes, -1)
    local = score(((0, 0), (0, 1)), (own_a, own_b), local)
    after_b, local = lax.optimization_barrier((after_b, local))
    with jax.named_scope("across"):
        across_a, across_b = shift(before_a, axes, 1), shift(after_b, axes, -1)
    local = score(((1, 0), (2, 1)), (before_a, after_b), local)
    before_b, after_a, local = lax.optimization_barrier((before_b, after_a, local))
    local = score(((1, 1), (2, 0)), (before_b, after_a), local)
    across_a, across_b, local = lax.optimization_barrier((across_a, across_b, local))
    local = score(((3, 0), (3, 1)), (across_a, across_b), local)
    spots = [spots[i, h] for i in range(SIDE) for h in range(2)]
    stats = local
    for axes, calls in zip(ORDERS, SWAPS):
        with jax.named_scope("core"):
            new = [to_core(theirs[c]) for c in calls]
        stats = merged([stats] + [shift(stats, axes, by) for by in (2, 1, -1)])
        stats, theirs, new = lax.optimization_barrier((stats, theirs, new))
        got += new
    factor = total_cent * jnp.exp(local[:, :SIDE] - (stats[:, :SIDE] + jnp.log(stats[:, SIDE:])))
    with jax.named_scope("core"):
        factors = factor, to_core(factor)
    out, sums, loads = weight_all(factors, ours, theirs, got, spots, total_rows)
    return out.reshape(8, 512, cent), sums, loads.reshape(cent)


def solution(mesh):
    placed = (P("blk", "shard", None), P(AXES, None), P(AXES))
    return jax.shard_map(
        per_device,
        mesh=mesh,
        in_specs=placed,
        out_specs=(P(None, None, AXES), P(AXES, None), P(AXES)),
        check_vma=False,
    )
```

```python
import functools
import math

import jax
import jax.numpy as jnp
from jax import lax
from jax.experimental import pallas as pl
from jax.experimental.pallas import tpu as pltpu
from jax.sharding import PartitionSpec as P

AXES = ("blk", "shard")
SIDE = 4
LANES = 128


def place_of(device):
    blk, shard = divmod(device, 32)
    return {"x": (shard & 1) * 2 + (blk >> 1), "y": (shard >> 1) & 3, "z": shard >> 3, "c": blk & 1}


def device_at(x, y, z, c):
    return ((x & 1) * 2 + c) * 32 + z * 8 + y * 2 + (x >> 1)


def along(axis0, axis1, by):
    pairs = []
    for device in range(128):
        place = place_of(device)
        axis = axis1 if place["c"] else axis0
        place[axis] = (place[axis] + by) % SIDE
        pairs.append((device, device_at(**place)))
    return pairs


def to_core(value):
    pairs = []
    for device in range(128):
        place = place_of(device)
        place["c"] = 1 - place["c"]
        pairs.append((device, device_at(**place)))
    return lax.ppermute(value, AXES, pairs)


def shift(value, axes, by):
    return lax.ppermute(value, AXES, along(*axes, by))


COST = 4
SWAPS = ((), (0, 1), (2, 3))
SLOTS = 3
SPLIT = 2
STEPS = (0, 1, -1, 2)
TURN = (0, 1, 3, 2)
ORDERS = (("x", "z"), ("y", "x"), ("z", "y"))


def spread(value, axes, here):
    out = jnp.zeros((SIDE,) + value.shape, value.dtype)
    out = lax.dynamic_update_index_in_dim(out, value, here, 0)
    for by in (2, 1, -1):
        got = shift(value, axes, by)
        out = lax.dynamic_update_index_in_dim(out, got, (here - by) % SIDE, 0)
    return out.reshape((SIDE * value.shape[0],) + value.shape[1:])


def places():
    blk, shard = lax.axis_index("blk"), lax.axis_index("shard")
    at = {"x": (shard & 1) * 2 + (blk >> 1), "y": (shard >> 1) & 3, "z": shard >> 3}
    return blk & 1, [[at[axes[kind]] for axes in ORDERS] for kind in range(2)]


def sources(place):
    return [(place[2] - by) & 3 for by in STEPS], [(place[1] + by) & 3 for by in TURN]


def in_vmem(value):
    return pltpu.with_memory_space_constraint(value, pltpu.VMEM)


def in_hbm(value):
    return pltpu.with_memory_space_constraint(value, pltpu.HBM)


def score_kernel(scale, units, rows_a, rows_b, cent_a, cent_b, bias_a, bias_b, before_ref, *refs):
    ours_ref, sent_ref, stat_ref, staged, part_sems, row_sems = refs
    cent, width = cent_a.shape
    size = rows_a.shape[0]
    core, place = places()
    lasts, mids = zip(*[sources(p) for p in place])
    lane = lax.broadcasted_iota(jnp.int32, (LANES, LANES), 1)
    copies = []
    for u, rows_ref in enumerate((rows_a, rows_b)):
        copy = pltpu.make_async_copy(
            rows_ref, sent_ref.at[u, :, pl.ds(cent, width)], row_sems.at[u]
        )
        copy.start()
        copies.append(copy)
    stat_ref[...] = before_ref[...]
    for u, rows_ref in enumerate((rows_a, rows_b)):
        piece, half = units[u]
        last = jnp.where(core == 0, lasts[0][piece], lasts[1][piece])
        scores = [
            lax.dot_general(
                rows_ref[...],
                cent_ref[...],
                (((1,), (1,)), ((), ())),
                preferred_element_type=jnp.float32,
            )
            * scale
            - bias_ref[...]
            for cent_ref, bias_ref in ((cent_a, bias_a), (cent_b, bias_b))
        ]
        for t in range(size // LANES):
            cut = slice(t * LANES, (t + 1) * LANES)
            top = jnp.max(jnp.maximum(scores[0][cut], scores[1][cut]), axis=1, keepdims=True)
            powers = [jnp.exp(score[cut] - top) for score in scores]
            staged[u, cut, :] = powers[0].astype(jnp.bfloat16)
            copy = pltpu.make_async_copy(
                staged.at[u, pl.ds(t * LANES, LANES)],
                ours_ref.at[u, pl.ds(t * LANES, LANES)],
                part_sems.at[u, t],
            )
            copy.start()
            copies.append(copy)
            sent_ref[u, cut, :cent] = powers[1].astype(jnp.bfloat16)
            total = jnp.sum(powers[0] + powers[1], axis=1, keepdims=True)
            flat = jnp.where(lane == 0, top, total).T
            turn = half * (size // LANES) + t
            row = jnp.where(core == 0, mids[0][turn], mids[1][turn])
            stat_ref[last, pl.ds(row, 1), :] = flat[0:1, :]
            stat_ref[last, pl.ds(SIDE + row, 1), :] = flat[1:2, :]
    for copy in copies:
        copy.wait()


def score_rows(units, rows, cents, biases, local, scale):
    size, width = rows[0].shape
    cent = cents[0].shape[0]
    vmem = pl.BlockSpec(memory_space=pltpu.VMEM)
    return pl.pallas_call(
        functools.partial(score_kernel, scale, units),
        out_shape=(
            pltpu.HBM((2, size, cent), jnp.bfloat16),
            pltpu.VMEM((2, size, cent + width), jnp.bfloat16),
            jax.ShapeDtypeStruct(local.shape, jnp.float32),
        ),
        in_specs=[vmem] * 7,
        out_specs=(pl.BlockSpec(memory_space=pl.ANY), vmem, vmem),
        scratch_shapes=[
            pltpu.VMEM((2, size, cent), jnp.bfloat16),
            pltpu.SemaphoreType.DMA((2, size // LANES)),
            pltpu.SemaphoreType.DMA((2,)),
        ],
        compiler_params=pltpu.CompilerParams(vmem_limit_bytes=14 * 2**20),
        cost_estimate=pl.CostEstimate(
            flops=int(COST * 8 * size * width * cent),
            bytes_accessed=int(COST * (4 * width * (size + cent) + 8 * size * cent)),
            transcendentals=int(COST * 4 * size * cent),
        ),
        name="scores",
    )(*[in_vmem(v) for v in (*rows, *cents, *biases)], local)


def weight_kernel(spots, total_rows, *refs):
    pieces = 2 * SIDE
    calls = len(spots) // 2
    factors, refs = refs[:2], refs[2:]
    ours, sent, got, refs = refs[:calls], refs[calls : 2 * calls], refs[2 * calls : 3 * calls], refs[3 * calls :]
    out_ref, sums_ref, loads_ref, *refs = refs
    parts, blocks, staged, rounded, sums, sems, part_sems, block_sems, sum_sems = refs
    order = [*range(SIDE, pieces), *range(SIDE)]
    tiles = SIDE
    cent = sums_ref.shape[0]
    half = parts.shape[1] // 2

    def fetches(i):
        if i >= SIDE:
            return ()
        moves = []
        for h in range(2):
            call, u = spots[2 * i + h]
            there = pl.ds(h * half, half)
            moves += [
                pltpu.make_async_copy(ours[call].at[u], parts.at[i, there], part_sems.at[i, h]),
                pltpu.make_async_copy(
                    sent[call].at[u, :, pl.ds(cent, blocks.shape[2])],
                    blocks.at[i, there],
                    block_sems.at[i, h],
                ),
            ]
        return moves

    def part_of(i, t):
        if i < SIDE:
            return parts[i, t * LANES : (t + 1) * LANES, :]
        call, u = spots[2 * (i - SIDE) + t * LANES // half]
        start = t * LANES % half
        return got[call][u, start : start + LANES, :cent]

    def block_of(i, cols):
        if i < SIDE:
            return blocks[i, :, cols]
        halves = [spots[2 * (i - SIDE) + h] for h in range(2)]
        there = slice(cent + cols.start, cent + cols.stop)
        return jnp.concatenate([got[call][u, :, there] for call, u in halves])

    for i in range(SIDE):
        for copy in fetches(i):
            copy.start()

    here, place = places()
    found = [sources(p) for p in place]

    def body(core):
        def sends(n):
            i, slot = order[n], n % SLOTS
            kind = core if i < SIDE else 1 - core
            last = found[kind][0][i % SIDE]
            for x_lo in range(2):
                for j in range(2):
                    if kind == 0:
                        there = out_ref.at[x_lo, 0, j, last]
                    else:
                        there = out_ref.at[x_lo, 1, j, :, last]
                    yield pltpu.make_async_copy(staged.at[slot, x_lo, j], there, sems.at[slot])

        def sum_copy(part):
            width = blocks.shape[2] // SPLIT
            cols = pl.ds(part * width, width)
            return pltpu.make_async_copy(sums.at[:, cols], sums_ref.at[:, cols], sum_sems.at[part])

        def add_sums(n, part):
            i = order[n]
            width = blocks.shape[2] // SPLIT
            cols = slice(part * width, (part + 1) * width)
            part_sums = lax.dot_general(
                rounded[n % 2],
                block_of(i, cols),
                (((0,), (0,)), ((), ())),
                preferred_element_type=jnp.float32,
            )
            if n == 0:
                sums[:, cols] = part_sums
            elif n + 1 < pieces:
                sums[:, cols] += part_sums
            else:
                sums[:, cols] = (sums[:, cols] + part_sums) * (1.0 / math.sqrt(total_rows))

        def weigh(n, t):
            i, slot = order[n], n % SLOTS
            kind = core if i < SIDE else 1 - core
            mid = found[kind][1][t]
            part = slice(t * LANES, (t + 1) * LANES)
            row = factors[i // SIDE][found[kind][0][i % SIDE], pl.ds(mid, 1), :]
            column = jnp.broadcast_to(row, (LANES, LANES)).T
            column = jnp.concatenate([column] * (cent // LANES), axis=1)
            weight = part_of(i, t).astype(jnp.float32) * column
            for p in range(SIDE):
                for j in range(2):
                    chunk = weight[(p * 2 + j) * 16 : (p * 2 + j) * 16 + 16]
                    if kind == 0:
                        staged[slot, p % 2, j, mid, p // 2] = chunk
                    else:
                        staged[slot, mid & 1, j, p, mid >> 1] = chunk
            rounded[n % 2, part, :] = weight.astype(jnp.bfloat16)
            return jnp.sum(weight.reshape(LANES // 8, 8, cent), axis=0)

        load = jnp.zeros((8, cent), jnp.float32)
        for n in range(pieces):
            if n >= SLOTS:
                for copy in sends(n - SLOTS):
                    copy.wait()
            for copy in fetches(order[n]):
                copy.wait()
            for t in range(tiles):
                load = load + weigh(n, t)
                if n and (t + 1) % (tiles // SPLIT) == 0:
                    add_sums(n - 1, t // (tiles // SPLIT))
            for copy in sends(n):
                copy.start()
        for part in range(SPLIT):
            add_sums(pieces - 1, part)
            sum_copy(part).start()
        loads_ref[...] = jnp.sum(load, axis=0, keepdims=True) * (1.0 / total_rows)
        for n in range(pieces - SLOTS, pieces):
            for copy in sends(n):
                copy.wait()
        for part in range(SPLIT):
            sum_copy(part).wait()

    for core in range(2):

        @pl.when(here == core)
        def _(core=core):
            body(core)


def weight_all(factors, ours, sent, got, spots, total_rows):
    _, size, cent = ours[0].shape
    height = 2 * size
    width = sent[0].shape[2] - cent
    vmem = pl.BlockSpec(memory_space=pltpu.VMEM)
    hbm = pl.BlockSpec(memory_space=pl.ANY)
    return pl.pallas_call(
        functools.partial(weight_kernel, spots, float(total_rows)),
        out_shape=(
            jax.ShapeDtypeStruct((2, 2, 2, 4, 4, 2, 16, cent), jnp.float32),
            jax.ShapeDtypeStruct((cent, width), jnp.float32),
            jax.ShapeDtypeStruct((1, cent), jnp.float32),
        ),
        in_specs=[vmem] * 2
        + [hbm] * (len(ours) + len(sent))
        + [vmem] * len(got),
        out_specs=(hbm, hbm, vmem),
        scratch_shapes=[
            pltpu.VMEM((SIDE, height, cent), jnp.bfloat16),
            pltpu.VMEM((SIDE, height, width), jnp.bfloat16),
            pltpu.VMEM((SLOTS, 2, 2, 4, 2, 16, cent), jnp.float32),
            pltpu.VMEM((2, height, cent), jnp.bfloat16),
            pltpu.VMEM((cent, width), jnp.float32),
            pltpu.SemaphoreType.DMA((SLOTS,)),
            pltpu.SemaphoreType.DMA((SIDE, 2)),
            pltpu.SemaphoreType.DMA((SIDE, 2)),
            pltpu.SemaphoreType.DMA((SPLIT,)),
        ],
        compiler_params=pltpu.CompilerParams(vmem_limit_bytes=20 * 2**20),
        name="weights",
    )(*factors, *[in_hbm(v) for v in (*ours, *sent)], *[in_vmem(v) for v in got])


def merged(stats):
    half = stats[0].shape[1] // 2
    tops = [s[:, :half] for s in stats]
    top = functools.reduce(jnp.maximum, tops)
    total = sum(s[:, half:] * jnp.exp(t - top) for s, t in zip(stats, tops))
    return jnp.concatenate([top, total], axis=1)


def per_device(embeddings, centroids, prices):
    core, place = places()
    first_place = jnp.where(core == 0, place[0][0], place[1][0])
    width = embeddings.shape[2]
    cent = centroids.shape[0]
    scale = 1.0 / math.sqrt(width)
    bias = (prices.astype(jnp.float32) / 1024.0).reshape(1, cent)
    with jax.named_scope("core"):
        cents, biases = (centroids, to_core(centroids)), (bias, to_core(bias))
    total_cent = cent * 128
    total_rows = embeddings.shape[0] * embeddings.shape[1] * 128

    first = spread(embeddings.reshape(-1, width), ORDERS[0], first_place)
    first, cents, biases = lax.optimization_barrier((first, cents, biases))
    with jax.named_scope("mid"):
        mids = [first] + [shift(first, ORDERS[1], -by if by < 3 else 1) for by in TURN[1:]]
    own_a, own_b = jnp.concatenate(mids[:2]), jnp.concatenate(mids[2:])
    axes = ORDERS[2]
    local = jnp.zeros((SIDE, 2 * SIDE, LANES), jnp.float32)
    ours, theirs, got, spots = [], [], [], {}

    def score(units, rows, local):
        our, their, local = score_rows(units, rows, cents, biases, local, scale)
        for u, unit in enumerate(units):
            spots[unit] = len(ours), u
        ours.append(our)
        theirs.append(their)
        return local

    with jax.named_scope("last"):
        before_a, after_b = shift(own_a, axes, 1), shift(own_b, axes, -1)
        before_b, after_a = shift(own_b, axes, 1), shift(own_a, axes, -1)
    local = score(((0, 0), (0, 1)), (own_a, own_b), local)
    after_b, local = lax.optimization_barrier((after_b, local))
    with jax.named_scope("across"):
        across_a, across_b = shift(before_a, axes, 1), shift(after_b, axes, -1)
    local = score(((1, 0), (2, 1)), (before_a, after_b), local)
    before_b, after_a, local = lax.optimization_barrier((before_b, after_a, local))
    local = score(((1, 1), (2, 0)), (before_b, after_a), local)
    across_a, across_b, local = lax.optimization_barrier((across_a, across_b, local))
    local = score(((3, 0), (3, 1)), (across_a, across_b), local)
    spots = [spots[i, h] for i in range(SIDE) for h in range(2)]
    stats = local
    for axes, calls in zip(ORDERS, SWAPS):
        with jax.named_scope("core"):
            new = [to_core(theirs[c]) for c in calls]
        stats = merged([stats] + [shift(stats, axes, by) for by in (2, 1, -1)])
        stats, theirs, new = lax.optimization_barrier((stats, theirs, new))
        got += new
    factor = total_cent * jnp.exp(local[:, :SIDE] - (stats[:, :SIDE] + jnp.log(stats[:, SIDE:])))
    with jax.named_scope("core"):
        factors = factor, to_core(factor)
    out, sums, loads = weight_all(factors, ours, theirs, got, spots, total_rows)
    return out.reshape(8, 512, cent), sums, loads.reshape(cent)


def solution(mesh):
    placed = (P("blk", "shard", None), P(AXES, None), P(AXES))
    return jax.shard_map(
        per_device,
        mesh=mesh,
        in_specs=placed,
        out_specs=(P(None, None, AXES), P(AXES, None), P(AXES)),
        check_vma=False,
    )
```
